32 devices in a mesh: grp: 2 (over y), op: 4 (over z), sec: 2 (over x), sub: 2 (over core).
Axes of the slice: x: 2, y: 2, z: 4, core: 2. Of those that a mesh axis runs over, the one named last changes fastest.
Arguments:
- wavefunction: float32 [16, 256, 256], P(('grp', 'sec'), None, 'sub'), parts along dimension 0, may hold values from -100 to 100
- diagonal: float32 [16, 256, 256], P(('grp', 'sec'), None, 'sub'), parts along dimension 0, may hold values from 0.5 to 10
- left_env: bfloat16 [192, 8, 256, 256], P(('grp', 'op'), 'sec'), parts along dimension 0, may hold values from -1 to 2
- right_env: bfloat16 [192, 8, 256, 256], P(('grp', 'op'), 'sec', 'sub'), parts along dimension 0, may hold values from -1 to 1
- targets: int32 [192, 8], P(('grp', 'op'), 'sec'), parts along dimension 0, may hold values from -1 to 7, as said below
Outputs:
- refined: float32 [16, 256, 256], P(('grp', 'sec'), None, 'sub'), parts along dimension 0
- ritz_values: float32 [4], P('grp'), parts along dimension 0
The draws below stay inside these ranges and needn't reach their ends.
There are 2 independent parts, one for each index of `grp`. The reference program is written for one: setup_inputs(seed, part) draws one part's arguments, and reference() takes and returns one part's arrays. A program takes and returns all parts, laid end to end along the dimension named above; each array names one. Nothing has to cross between parts.
Inputs may be any that keep to these rules, and one draw needn't show every extreme that they name: `targets`: -1 marks a term that does not act on the block; any other value is the block that receives its image.
All inputs are finite; a program needn't handle non-finite values.
Results may differ from the reference program's by a relative error of at most 0.0029.
Values sent between devices are 32-bit elements; how exact they have to be, the bound alone decides.
No kernel may reach another device: no remote copies, remote signals or barrier semaphores. Data moves between devices by JAX's collectives and lax.ppermute only.
A program may use at most 128 MiB of HBM per device.

```python
import math
import jax
import jax.numpy as jnp
from jax import lax

TILE = 256
ITERS = 2
NBLK = 8
TERMS = 96


def draw_wavefunction(key, part):
    key = jax.random.fold_in(key, 11)
    first, second, third = jax.random.split(key, 3)
    ramp = jnp.sqrt(1.0 + 2.0 * jnp.arange(NBLK, dtype=jnp.float32) / max(NBLK - 1, 1))
    base = jnp.clip(jax.random.normal(first, (NBLK, TILE, TILE), jnp.float32), -4.0, 4.0)
    reach = math.log(10.0)
    rows = jnp.exp(jax.random.uniform(second, (NBLK, TILE, 1), jnp.float32, 0.0, reach))
    columns = jnp.exp(jax.random.uniform(third, (NBLK, 1, TILE), jnp.float32, 0.0, reach))
    return (base * ramp[:, None, None] * rows * columns / 10.0).astype(jnp.float32)


def draw_diagonal(key, part):
    key = jax.random.fold_in(key, 12)
    first = jax.random.fold_in(key, 0)
    ramp = 1.0 + 2.0 * jnp.arange(NBLK, dtype=jnp.float32) / max(NBLK - 1, 1)
    rough = jnp.exp(jax.random.uniform(first, (NBLK, TILE, TILE), jnp.float32, 0.0, math.log(3.0)))
    return (ramp[:, None, None] * rough).astype(jnp.float32)


def draw_left_env(key, part):
    key = jax.random.fold_in(key, 13)
    first, second = jax.random.split(key, 2)
    spread = 1.0 / math.sqrt(TILE)
    shape = (TERMS, NBLK, TILE, TILE)
    noise = jnp.clip(jax.random.normal(first, shape, jnp.float32), -4.0, 4.0) * spread
    weight_diag = jax.random.uniform(second, (TERMS, NBLK, 1, 1), jnp.float32, 0.25, 0.75)
    identity = jnp.eye(TILE, dtype=jnp.float32)
    return (noise + weight_diag * identity).astype(jnp.bfloat16)


def draw_right_env(key, part):
    key = jax.random.fold_in(key, 15)
    first, second = jax.random.split(key, 2)
    spread = 1.0 / math.sqrt(TILE * TERMS)
    shape = (TERMS, NBLK, TILE, TILE)
    noise = jnp.clip(jax.random.normal(first, shape, jnp.float32), -4.0, 4.0) * spread
    weight_diag = jax.random.uniform(second, (TERMS, NBLK, 1, 1), jnp.float32, 0.5, 1.5)
    identity = jnp.eye(TILE, dtype=jnp.float32)
    return (noise + weight_diag * (4.0 / TERMS) * identity).astype(jnp.bfloat16)


def draw_targets(key, part):
    key = jax.random.fold_in(key, 14)
    first, second = jax.random.split(key, 2)
    own = jnp.broadcast_to(jnp.arange(NBLK, dtype=jnp.int32)[None, :], (TERMS, NBLK))
    other = jax.random.randint(first, (TERMS, NBLK), -1, NBLK).astype(jnp.int32)
    keep = jax.random.randint(second, (TERMS, NBLK), 0, 2).astype(jnp.int32)
    result = jnp.where(keep == 1, own, other).astype(jnp.int32)
    result = result.at[0, NBLK - 1].set(NBLK - 1)
    result = result.at[TERMS - 1, 0].set(-1)
    return result.astype(jnp.int32)


def setup_inputs(seed: int = 0, part: int = 0) -> dict:
    arg_keys = jax.random.split(jax.random.key(seed), 6)
    own_keys = jax.random.split(jax.random.fold_in(arg_keys[5], part), 6)
    wavefunction = draw_wavefunction(jax.random.fold_in(jax.random.fold_in(arg_keys[5], part), 71), part)
    diagonal = draw_diagonal(jax.random.fold_in(jax.random.fold_in(arg_keys[5], part), 71), part)
    left_env = draw_left_env(jax.random.fold_in(jax.random.fold_in(arg_keys[5], part), 71), part)
    right_env = draw_right_env(jax.random.fold_in(jax.random.fold_in(arg_keys[5], part), 71), part)
    targets = draw_targets(jax.random.fold_in(jax.random.fold_in(arg_keys[5], part), 71), part)
    return {"wavefunction": wavefunction, "diagonal": diagonal, "left_env": left_env, "right_env": right_env, "targets": targets}


def inner_mean(first, second):
    return jnp.sum(first * second) / (NBLK * TILE * TILE)

def apply_terms(vector, left_env, right_env, targets):
    vector_bf = lax.optimization_barrier(vector.astype(jnp.bfloat16)).astype(jnp.float32)
    labels = jnp.arange(NBLK, dtype=jnp.int32)

    def accumulate(total, pieces):
        left_term, right_term, target_row = pieces
        product = jnp.einsum('bij,bjk->bik', left_term.astype(jnp.float32), vector_bf, precision=lax.Precision.HIGHEST)
        product = lax.optimization_barrier(product.astype(jnp.bfloat16)).astype(jnp.float32)
        image = jnp.einsum('bik,bkl->bil', product, right_term.astype(jnp.float32), precision=lax.Precision.HIGHEST)
        onehot = (target_row[:, None] == labels[None, :]).astype(jnp.float32)
        return (total + jnp.einsum('bn,bil->nil', onehot, image, precision=lax.Precision.HIGHEST), None)
    total, _ = lax.scan(accumulate, jnp.zeros((NBLK, TILE, TILE), jnp.float32), (left_env, right_env, targets))
    return total

def reference(wavefunction, diagonal, left_env, right_env, targets):
    vector = wavefunction / jnp.sqrt(inner_mean(wavefunction, wavefunction))
    ritz_list = []
    for turn_index in range(ITERS):
        sigma = diagonal * vector + apply_terms(vector, left_env, right_env, targets)
        theta = inner_mean(vector, sigma)
        correction = (sigma - theta * vector) / (1.0 + jnp.abs(diagonal - theta))
        along = inner_mean(vector, correction)
        updated = vector - (correction - along * vector)
        vector = updated / jnp.sqrt(inner_mean(updated, updated))
        ritz_list.append(theta)
    return (vector, jnp.stack(ritz_list))
```

```python
import functools

import jax
import jax.numpy as jnp
from jax import lax
from jax.experimental import pallas as pl
from jax.experimental.pallas import tpu as pltpu
from jax.sharding import PartitionSpec as P

ITERS = 2
GROUP = 2
SLOTS = 10
REMOTE, OWN = 0, 1
VMEM = pl.BlockSpec(memory_space=pltpu.VMEM)
SMEM = pl.BlockSpec(memory_space=pltpu.SMEM)
ANY = pl.BlockSpec(memory_space=pl.ANY)


def f32(*shape):
    return jax.ShapeDtypeStruct(shape, jnp.float32)


def i32(*shape):
    return jax.ShapeDtypeStruct(shape, jnp.int32)


def step_cap(pairs, slots):
    steps = (pairs + slots) // 2 + GROUP
    return -(-steps // GROUP) * GROUP


def plan_kernel(secs, cap, targets, wave, tile, block, slot, groups, square, fill):
    terms, blocks = targets.shape
    total = secs * blocks
    my_sec = lax.axis_index("sec")

    def clear(index, carry):
        tile[index] = 0
        block[index] = blocks
        return carry

    lax.fori_loop(0, 4 * cap, clear, 0)
    lax.fori_loop(0, 2 * cap, lambda index, carry: (slot.__setitem__(index, 0), carry)[1], 0)
    for index in range(total + 1):
        fill[index] = 0

    def relative(target):
        owner = lax.div(jnp.maximum(target, 0), blocks)
        turn = owner - my_sec
        turn = jnp.where(turn < 0, turn + secs, turn)
        place = turn * blocks + (target - owner * blocks)
        return jnp.where(target < 0, total, place)

    def count(term, carry):
        for b in range(blocks):
            place = relative(targets[term, b])
            fill[place] = fill[place] + 1
        return carry

    lax.fori_loop(0, terms, count, 0)

    for region, places in ((REMOTE, range(blocks, total)), (OWN, range(blocks))):
        step = jnp.int32(region * cap)
        for place in places:
            steps = lax.div(fill[place] + 1, 2)

            def mark(index, carry, place=place, places=places):
                slot[index] = place - places[0]
                return carry

            lax.fori_loop(step, step + steps, mark, 0)
            fill[place] = 2 * step
            step = step + steps
        groups[region] = lax.div(step - region * cap + GROUP - 1, GROUP)
    fill[total] = 4 * cap

    def place_pairs(term, carry):
        for b in range(blocks):
            place = relative(targets[term, b])
            at = fill[place]
            fill[place] = at + 1
            tile[at] = term * blocks + b
            block[at] = b
        return carry

    lax.fori_loop(0, terms, place_pairs, 0)
    square[0, 0] = jnp.sum(wave[...] * wave[...])


def plan(targets, wave, secs):
    terms, blocks = targets.shape
    pairs = terms * blocks
    cap = step_cap(pairs, secs * blocks)
    return pl.pallas_call(
        functools.partial(plan_kernel, secs, cap),
        out_shape=(i32(4 * cap + pairs), i32(4 * cap + pairs), i32(2 * cap), i32(2), f32(1, 1)),
        in_specs=[SMEM, VMEM],
        out_specs=(SMEM,) * 5,
        scratch_shapes=[pltpu.SMEM((secs * blocks + 1,), jnp.int32)],
        name="plan",
    )(targets, wave)


def terms_kernel(
    region, cap, tile, block, slot, groups, vector, left, right, keep, send,
    vector_bf, left_buf, right_buf, product, total, left_sem, right_sem, out_sem,
):
    blocks = vector.shape[0]
    my_sub = lax.axis_index("sub")
    many = 2 * GROUP
    count = groups[region]

    def fetch(group, carry):
        buf = lax.rem(group, SLOTS)
        for k in range(many):
            pair = tile[2 * region * cap + group * many + k]
            pltpu.make_async_copy(left.at[pair], left_buf.at[buf, k], left_sem.at[buf]).start()
            pltpu.make_async_copy(right.at[pair], right_buf.at[buf, k], right_sem.at[buf]).start()
        return carry

    def arrive(group):
        buf = lax.rem(group, SLOTS)
        pltpu.make_async_copy(left_buf.at[buf], left_buf.at[buf], left_sem.at[buf]).wait()
        pltpu.make_async_copy(right_buf.at[buf], right_buf.at[buf], right_sem.at[buf]).wait()

    def first(group):
        buf = lax.rem(group, SLOTS)
        for k in range(many):
            b = block[2 * region * cap + group * many + k]
            part = jnp.dot(left_buf[buf, k], vector_bf[b], preferred_element_type=jnp.float32)
            half = part.shape[1]
            product[k // 2, :, (k % 2) * half : (k % 2 + 1) * half] = part.astype(jnp.bfloat16)

    def second(group):
        buf = lax.rem(group, SLOTS)
        for g in range(GROUP):
            n = slot[region * cap + group * GROUP + g]
            pair = right_buf[buf, 2 * g : 2 * g + 2]
            pair = pair.reshape(2 * pair.shape[1], pair.shape[2])
            image = jnp.dot(product[g], pair, preferred_element_type=jnp.float32)
            half = image.shape[1] // 2
            total[0, n] += image[:, :half]
            total[1, n] += image[:, half:]

    lax.fori_loop(0, jnp.minimum(count, SLOTS), fetch, 0)
    vector_bf[:blocks] = vector[...].astype(jnp.bfloat16)
    vector_bf[blocks] = jnp.zeros(vector_bf.shape[1:], jnp.bfloat16)
    total[...] = jnp.zeros_like(total)

    @pl.when(count > 0)
    def _():
        arrive(0)
        first(0)

        def turn(group, carry):
            arrive(group)
            second(group - 1)
            first(group)

            @pl.when(group - 1 + SLOTS < count)
            def _():
                fetch(group - 1 + SLOTS, 0)

            return carry

        lax.fori_loop(1, count, turn, 0)
        second(count - 1)

    kept = pltpu.make_async_copy(total.at[my_sub], keep, out_sem.at[0])
    sent = pltpu.make_async_copy(total.at[1 - my_sub], send, out_sem.at[1])
    sent.start()
    kept.start()
    sent.wait()
    kept.wait()


def term_images(region, slots, planned, vector, left, right):
    tile, block, slot, groups, cap = planned
    blocks, rows, half = vector.shape
    many = 2 * GROUP
    return pl.pallas_call(
        functools.partial(terms_kernel, region, cap),
        out_shape=(f32(slots, rows, half), f32(slots, rows, half)),
        in_specs=[SMEM] * 4 + [VMEM, ANY, ANY],
        out_specs=(ANY, ANY),
        scratch_shapes=[
            pltpu.VMEM((blocks + 1, rows, half), jnp.bfloat16),
            pltpu.VMEM((SLOTS, many, rows, rows), jnp.bfloat16),
            pltpu.VMEM((SLOTS, many, half, rows), jnp.bfloat16),
            pltpu.VMEM((GROUP, rows, rows), jnp.bfloat16),
            pltpu.VMEM((2, slots, rows, half), jnp.float32),
            pltpu.SemaphoreType.DMA((SLOTS,)),
            pltpu.SemaphoreType.DMA((SLOTS,)),
            pltpu.SemaphoreType.DMA((2,)),
        ],
        compiler_params=pltpu.CompilerParams(vmem_limit_bytes=24 * 1024 * 1024),
        cost_estimate=pl.CostEstimate(flops=10**9, bytes_accessed=9 * 2**20, transcendentals=0),
        name="remote_images" if region == REMOTE else "own_images",
    )(tile, block, slot, groups, vector, left, right)


def add_kernel(a, b, out):
    out[...] = a[...] + b[...]


def add(a, b):
    return pl.pallas_call(
        add_kernel, out_shape=f32(*a.shape), in_specs=[VMEM] * 2, out_specs=VMEM, name="add"
    )(a, b)


def combine_kernel(arrived, vector, diagonal, *refs):
    parts, outs, inner = refs[:arrived], refs[arrived:-1], refs[-1]
    ops = len(outs)
    my_op = lax.axis_index("op")
    inner_sum = jnp.float32(0)
    for turn in range(ops):
        at = lax.rem(my_op + turn, ops)
        total = parts[0][at]
        for part in parts[1:]:
            total = total + part[at]
        outs[turn][...] = total
        held = vector[at]
        if turn == 0:
            inner_sum += jnp.sum(held * (diagonal[at] * held + total))
        else:
            inner_sum += jnp.sum(held * total)
    inner[0, 0] = inner_sum


def combine(vector, diagonal, parts):
    ops, rows, half = vector.shape
    outs = pl.pallas_call(
        functools.partial(combine_kernel, len(parts)),
        out_shape=(f32(rows, half),) * ops + (f32(1, 1),),
        in_specs=[VMEM] * (2 + len(parts)),
        out_specs=(VMEM,) * ops + (SMEM,),
        name="combine",
    )(vector, diagonal, *parts)
    return outs[:-1], outs[-1]


def correct_kernel(entries, theta_sum, vector, diagonal, *refs):
    parts, (correction, sums) = refs[:-2], refs[-2:]
    my_op = lax.axis_index("op")
    theta = theta_sum[0, 0] / entries
    held, diag = vector[my_op], diagonal[my_op]
    sigma = diag * held
    for part in parts:
        sigma = sigma + part[...]
    value = (sigma - theta * held) / (1.0 + jnp.abs(diag - theta))
    correction[...] = value
    sums[0, 0] = jnp.sum(held * value)
    sums[0, 1] = jnp.sum(value * value)
    sums[0, 2] = jnp.sum(held * held)


def correct(entries, theta_sum, vector, diagonal, parts):
    ops, rows, half = vector.shape
    return pl.pallas_call(
        functools.partial(correct_kernel, entries),
        out_shape=(f32(rows, half), f32(1, 3)),
        in_specs=[SMEM] + [VMEM] * (2 + len(parts)),
        out_specs=(VMEM, SMEM),
        name="correct",
    )(theta_sum, vector, diagonal, *parts)


def refine_kernel(entries, sums, vector, *refs):
    parts, out = refs[:-1], refs[-1]
    ops = len(parts)
    my_op = lax.axis_index("op")
    shape = parts[0].shape
    along = jnp.full(shape, sums[0, 0] / entries)
    square = jnp.full(shape, sums[0, 1] / entries)
    own = jnp.full(shape, sums[0, 2] / entries)
    length_sq = (1.0 + along) * (1.0 + along) * own - 2.0 * (1.0 + along) * along + square
    length = jnp.sqrt(length_sq)
    for turn in range(ops):
        at = lax.rem(my_op + ops - turn, ops)
        held = vector[at]
        out[at] = (held - (parts[turn][...] - along * held)) / length


def refine(entries, sums, vector, parts):
    return pl.pallas_call(
        functools.partial(refine_kernel, entries),
        out_shape=f32(*vector.shape),
        in_specs=[SMEM] + [VMEM] * (1 + len(parts)),
        out_specs=VMEM,
        name="refine",
    )(sums, vector, *parts)


def shift(array, axis, turn):
    count = lax.axis_size(axis)
    return lax.ppermute(array, axis, [(i, (i + turn) % count) for i in range(count)])


def per_device(wavefunction, diagonal, left_env, right_env, targets):
    ops, secs = lax.axis_size("op"), lax.axis_size("sec")
    blocks, tile, half = wavefunction.shape
    terms = left_env.shape[0]
    entries = blocks * secs * tile * tile
    left = left_env.reshape(terms * blocks, tile, tile)
    right = right_env.reshape(terms * blocks, half, tile)
    split = (ops, blocks * tile // ops, half)
    *lists, square = plan(targets, wavefunction, secs)
    planned = (*lists, step_cap(terms * blocks, secs * blocks))
    start = lax.psum(square, ("sec", "sub"))
    vector = wavefunction / jnp.sqrt(start[0, 0] / entries)
    diagonal = diagonal.reshape(split)
    ritz_list = []
    for turn_index in range(ITERS):
        keep, send = term_images(REMOTE, (secs - 1) * blocks, planned, vector, left, right)
        remote = add(keep, shift(send, "sub", 1))
        arrived = [shift(remote[(r - 1) * blocks : r * blocks], "sec", r) for r in range(1, secs)]
        keep, send = term_images(OWN, blocks, planned, vector, left, right)
        parts = [keep, shift(send, "sub", 1), *arrived]
        vector = vector.reshape(split)
        pieces, inner = combine(vector, diagonal, [part.reshape(split) for part in parts])
        landed = [shift(pieces[k], "op", k) for k in range(1, ops)]
        theta_sum = lax.psum(inner, ("op", "sec", "sub"))
        correction, sums = correct(entries, theta_sum, vector, diagonal, [pieces[0], *landed])
        spread = [correction, *[shift(correction, "op", k) for k in range(1, ops)]]
        sums = lax.psum(sums, ("op", "sec", "sub"))
        vector = refine(entries, sums, vector, spread).reshape(blocks, tile, half)
        ritz_list.append(theta_sum[0, 0] / entries)
    return (vector, jnp.stack(ritz_list))


def solution(mesh):
    placed = (
        P(("grp", "sec"), None, "sub"),
        P(("grp", "sec"), None, "sub"),
        P(("grp", "op"), "sec", None, None),
        P(("grp", "op"), "sec", "sub", None),
        P(("grp", "op"), "sec"),
    )
    return jax.shard_map(
        per_device,
        mesh=mesh,
        in_specs=placed,
        out_specs=(P(("grp", "sec"), None, "sub"), P("grp")),
        check_vma=False,
    )
```

```python
import functools

import jax
import jax.numpy as jnp
from jax import lax
from jax.experimental import pallas as pl
from jax.experimental.pallas import tpu as pltpu
from jax.sharding import PartitionSpec as P

ITERS = 2
GROUP = 4
REMOTE, OWN = 0, 1
VMEM = pl.BlockSpec(memory_space=pltpu.VMEM)
SMEM = pl.BlockSpec(memory_space=pltpu.SMEM)


def f32(*shape):
    return jax.ShapeDtypeStruct(shape, jnp.float32)


def limit(mebibytes):
    return pltpu.CompilerParams(vmem_limit_bytes=mebibytes * 2**20)


def step_cap(pairs, slots):
    steps = (pairs + slots) // 2 + GROUP
    return -(-steps // GROUP) * GROUP


def list_places(pairs, slots):
    cap = step_cap(pairs, slots)
    block = 4 * cap + pairs
    slot = 2 * block
    groups = slot + 2 * cap
    return cap, block, slot, groups, groups + 2


def plan_kernel(secs, places, targets, wave, lists, square, fill):
    terms, blocks = targets.shape
    total = secs * blocks
    cap, block, slot, groups, _ = places
    my_sec = lax.axis_index("sec")

    def clear(index, carry):
        lists[index] = 0
        lists[block + index] = blocks
        return carry

    def clear_slot(index, carry):
        lists[slot + index] = 0
        return carry

    lax.fori_loop(0, 4 * cap, clear, 0)
    lax.fori_loop(0, 2 * cap, clear_slot, 0)
    for index in range(total + 1):
        fill[index] = 0

    def relative(target):
        owner = lax.div(jnp.maximum(target, 0), blocks)
        turn = owner - my_sec
        turn = jnp.where(turn < 0, turn + secs, turn)
        place = turn * blocks + (target - owner * blocks)
        return jnp.where(target < 0, total, place)

    def count(term, carry):
        for b in range(blocks):
            place = relative(targets[term, b])
            fill[place] = fill[place] + 1
        return carry

    lax.fori_loop(0, terms, count, 0)

    for region, span in ((REMOTE, range(blocks, total)), (OWN, range(blocks))):
        step = jnp.int32(region * cap)
        for place in span:
            steps = lax.div(fill[place] + 1, 2)

            def mark(index, carry, value=place - span[0]):
                lists[slot + index] = value
                return carry

            lax.fori_loop(step, step + steps, mark, 0)
            fill[place] = 2 * step
            step = step + steps
        lists[groups + region] = lax.div(step - region * cap + GROUP - 1, GROUP)
    fill[total] = 4 * cap

    def place_pairs(term, carry):
        for b in range(blocks):
            place = relative(targets[term, b])
            at = fill[place]
            fill[place] = at + 1
            lists[at] = term * blocks + b
            lists[block + at] = b
        return carry

    lax.fori_loop(0, terms, place_pairs, 0)
    square[...] = jnp.full(square.shape, jnp.sum(wave[...] * wave[...]))


def plan(targets, wave, secs):
    terms, blocks = targets.shape
    places = list_places(terms * blocks, secs * blocks)
    return pl.pallas_call(
        functools.partial(plan_kernel, secs, places),
        out_shape=(jax.ShapeDtypeStruct((places[-1],), jnp.int32), f32(8, 128)),
        in_specs=[SMEM, VMEM],
        out_specs=(SMEM, VMEM),
        scratch_shapes=[pltpu.SMEM((secs * blocks + 1,), jnp.int32)],
        compiler_params=limit(2),
        name="plan",
    )(targets, wave)


def added(refs):
    total = refs[0][...]
    for ref in refs[1:]:
        total = total + ref[...]
    return total


def multiply_terms(region, places, lists, left, right, vector_bf, product, keep, send):
    cap, block, slot, groups, _ = places
    my_sub = lax.axis_index("sub")
    many = 2 * GROUP
    half = keep.shape[2]
    count = lists[groups + region]
    keep[...] = jnp.zeros_like(keep)
    send[...] = jnp.zeros_like(send)

    def first(group):
        for k in range(many):
            at = 2 * region * cap + group * many + k
            part = jnp.dot(
                left[lists[at]], vector_bf[lists[block + at]], preferred_element_type=jnp.float32
            )
            product[k // 2, :, (k % 2) * half : (k % 2 + 1) * half] = part.astype(jnp.bfloat16)

    def second(group):
        for g in range(GROUP):
            at = region * cap + group * GROUP + g
            pair = jnp.concatenate([right[lists[2 * at]], right[lists[2 * at + 1]]], axis=0)
            image = jnp.dot(product[g], pair, preferred_element_type=jnp.float32)
            low, high = image[:, :half], image[:, half:]
            n = lists[slot + at]
            keep[n] += jnp.where(my_sub == 0, low, high)
            send[n] += jnp.where(my_sub == 0, high, low)

    @pl.when(count > 0)
    def _():
        first(0)

        def turn(group, carry):
            second(group - 1)
            first(group)
            return carry

        lax.fori_loop(1, count, turn, 0)
        second(count - 1)


def round_vector(vector, vector_bf):
    blocks = vector.shape[0]
    vector_bf[:blocks] = vector[...].astype(jnp.bfloat16)
    vector_bf[blocks] = jnp.zeros(vector_bf.shape[1:], jnp.bfloat16)


def start_kernel(entries, norms, places, lists, wave, *refs):
    norm_refs, (left, right, vector, keep, send, vector_bf, product) = refs[:norms], refs[norms:]
    length = jnp.sqrt(added(norm_refs)[:1, :1] / entries)
    vector[...] = wave[...] / length[None]
    round_vector(vector, vector_bf)
    multiply_terms(REMOTE, places, lists, left, right, vector_bf, product, keep, send)


def refined(entries, held_ref, sum_refs, parts, out):
    ops = len(parts)
    my_op = lax.axis_index("op")
    sums = added(sum_refs) / entries
    along, square, own = sums[0:1, :1], sums[1:2, :1], sums[2:3, :1]
    length = jnp.sqrt((1.0 + along) * (1.0 + along) * own - 2.0 * (1.0 + along) * along + square)
    rows = out.shape[0] * out.shape[1] // ops
    each = max(rows, out.shape[1])
    for turn in range(ops):
        place = lax.rem(my_op + ops - turn, ops)
        if rows >= out.shape[1]:
            at = pl.ds(place * (rows // out.shape[1]), rows // out.shape[1])
            held = held_ref[at]
            value = parts[turn][...].reshape(held.shape)
            out[at] = (held - (value - along[None] * held)) / length[None]
        else:
            share = out.shape[1] // rows
            at = (lax.div(place, share), pl.ds(pl.multiple_of(lax.rem(place, share) * rows, rows), rows))
            held = held_ref[at]
            out[at] = (held - (parts[turn][...] - along * held)) / length


def resume_kernel(entries, sums, ops, places, lists, held, *refs):
    sum_refs, parts, refs = refs[:sums], refs[sums : sums + ops], refs[sums + ops :]
    left, right, vector, keep, send, vector_bf, product = refs
    refined(entries, held, sum_refs, parts, vector)
    round_vector(vector, vector_bf)
    multiply_terms(REMOTE, places, lists, left, right, vector_bf, product, keep, send)


def own_kernel(places, lists, vector, left, right, keep, send, vector_bf, product):
    round_vector(vector, vector_bf)
    multiply_terms(OWN, places, lists, left, right, vector_bf, product, keep, send)


def images(kernel, slots, with_vector, name, lists, *operands):
    right = operands[-1]
    half, rows = right.shape[1:]
    vector = operands[0]
    out = (f32(slots, rows, half),) * 2
    if with_vector:
        out = (f32(*vector.shape), *out)
    return pl.pallas_call(
        kernel,
        out_shape=out,
        in_specs=[SMEM] + [VMEM] * len(operands),
        out_specs=(VMEM,) * len(out),
        scratch_shapes=[
            pltpu.VMEM((vector.shape[0] + 1, rows, half), jnp.bfloat16),
            pltpu.VMEM((GROUP, rows, rows), jnp.bfloat16),
        ],
        compiler_params=limit(28),
        cost_estimate=pl.CostEstimate(flops=10**9, bytes_accessed=9 * 2**20, transcendentals=0),
        name=name,
    )(lists, *operands)


def add_kernel(*refs):
    refs[-1][...] = added(refs[:-1])


def add(*parts):
    return pl.pallas_call(
        add_kernel,
        out_shape=f32(*parts[0].shape),
        in_specs=[VMEM] * len(parts),
        out_specs=VMEM,
        compiler_params=limit(6),
        name="add",
    )(*parts)


def combine_kernel(arrived, vector, diagonal, *refs):
    parts, outs, inner = refs[:arrived], refs[arrived:-1], refs[-1]
    ops = len(outs)
    my_op = lax.axis_index("op")
    inner_sum = jnp.float32(0)
    for turn in range(ops):
        at = lax.rem(my_op + turn, ops)
        total = parts[0][at]
        for part in parts[1:]:
            total = total + part[at]
        outs[turn][...] = total
        held = vector[at]
        if turn == 0:
            inner_sum += jnp.sum(held * (diagonal[at] * held + total))
        else:
            inner_sum += jnp.sum(held * total)
    inner[...] = jnp.full(inner.shape, inner_sum)


def combine(vector, diagonal, parts):
    ops, rows, half = vector.shape
    outs = pl.pallas_call(
        functools.partial(combine_kernel, len(parts)),
        out_shape=(f32(rows, half),) * ops + (f32(8, 128),),
        in_specs=[VMEM] * (2 + len(parts)),
        out_specs=(VMEM,) * (ops + 1),
        compiler_params=limit(8),
        name="combine",
    )(vector, diagonal, *parts)
    return outs[:-1], outs[-1]


def correct_kernel(entries, thetas, vector, diagonal, *refs):
    theta_refs, parts, (correction, sums, ritz) = refs[:thetas], refs[thetas:-3], refs[-3:]
    my_op = lax.axis_index("op")
    ritz[...] = added(theta_refs) / entries
    theta = ritz[:1, :1]
    held, diag = vector[my_op], diagonal[my_op]
    sigma = diag * held + added(parts)
    value = (sigma - theta * held) / (1.0 + jnp.abs(diag - theta))
    correction[...] = value
    sums[...] = jnp.zeros_like(sums)
    sums[0:1] = jnp.full((1, 128), jnp.sum(held * value))
    sums[1:2] = jnp.full((1, 128), jnp.sum(value * value))
    sums[2:3] = jnp.full((1, 128), jnp.sum(held * held))


def correct(entries, thetas, vector, diagonal, parts):
    ops, rows, half = vector.shape
    return pl.pallas_call(
        functools.partial(correct_kernel, entries, len(thetas)),
        out_shape=(f32(rows, half), f32(8, 128), f32(8, 128)),
        in_specs=[VMEM] * (2 + len(thetas) + len(parts)),
        out_specs=(VMEM,) * 3,
        compiler_params=limit(4),
        name="correct",
    )(vector, diagonal, *thetas, *parts)


def finish_kernel(entries, sums, held, *refs):
    refined(entries, held, refs[:sums], refs[sums:-1], refs[-1])


def finish(entries, vector, sums, spread):
    return pl.pallas_call(
        functools.partial(finish_kernel, entries, len(sums)),
        out_shape=f32(*vector.shape),
        in_specs=[VMEM] * (1 + len(sums) + len(spread)),
        out_specs=VMEM,
        compiler_params=limit(4),
        name="finish",
    )(vector, *sums, *spread)


def shift(array, axis, turn):
    count = lax.axis_size(axis)
    return lax.ppermute(array, axis, [(i, (i + turn) % count) for i in range(count)])


def from_all(array, axis):
    return [array, *[shift(array, axis, k) for k in range(1, lax.axis_size(axis))]]


def per_device(wavefunction, diagonal, left_env, right_env, targets):
    ops, secs = lax.axis_size("op"), lax.axis_size("sec")
    blocks, tile, half = wavefunction.shape
    terms = left_env.shape[0]
    entries = blocks * secs * tile * tile
    left = left_env.reshape(terms * blocks, tile, tile)
    right = right_env.reshape(terms * blocks, half, tile)
    split = (ops, blocks * tile // ops, half)
    places = list_places(terms * blocks, secs * blocks)
    lists, square = plan(targets, wavefunction, secs)
    away = (secs - 1) * blocks
    split_diagonal = diagonal.reshape(split)
    norms = from_all(square, ("sec", "sub"))
    start = functools.partial(start_kernel, entries, len(norms), places)
    vector, keep, send = images(start, away, True, "remote_images", lists, wavefunction, *norms, left, right)
    ritz_list = []
    for turn_index in range(ITERS):
        remote = add(keep, shift(send, "sub", 1))
        arrived = [shift(remote[(r - 1) * blocks : r * blocks], "sec", r) for r in range(1, secs)]
        own = functools.partial(own_kernel, places)
        keep, send = images(own, blocks, False, "own_images", lists, vector, left, right)
        parts = [keep, shift(send, "sub", 1), *arrived]
        held = vector.reshape(split)
        pieces, inner = combine(held, split_diagonal, [part.reshape(split) for part in parts])
        inner = add(*from_all(inner, ("sec", "sub")))
        thetas = from_all(inner, "op")
        landed = [shift(pieces[k], "op", k) for k in range(1, ops)]
        correction, sums, ritz = correct(entries, thetas, held, split_diagonal, [pieces[0], *landed])
        ritz_list.append(ritz[0, 0])
        sums = add(*from_all(sums, ("sec", "sub")))
        sums = from_all(sums, "op")
        spread = from_all(correction, "op")
        if turn_index < ITERS - 1:
            resume = functools.partial(resume_kernel, entries, len(sums), ops, places)
            vector, keep, send = images(
                resume, away, True, "remote_images", lists, vector, *sums, *spread, left, right
            )
        else:
            vector = finish(entries, vector, sums, spread)
    return (vector, jnp.stack(ritz_list))


def solution(mesh):
    placed = (
        P(("grp", "sec"), None, "sub"),
        P(("grp", "sec"), None, "sub"),
        P(("grp", "op"), "sec", None, None),
        P(("grp", "op"), "sec", "sub", None),
        P(("grp", "op"), "sec"),
    )
    return jax.shard_map(
        per_device,
        mesh=mesh,
        in_specs=placed,
        out_specs=(P(("grp", "sec"), None, "sub"), P("grp")),
        check_vma=False,
    )
```

```python
import functools

import jax
import jax.numpy as jnp
from jax import lax
from jax.experimental import pallas as pl
from jax.experimental.pallas import tpu as pltpu
from jax.sharding import PartitionSpec as P

ITERS = 2
GROUP = 4
REMOTE, OWN = 0, 1
VMEM = pl.BlockSpec(memory_space=pltpu.VMEM)
SMEM = pl.BlockSpec(memory_space=pltpu.SMEM)
ANY = pl.BlockSpec(memory_space=pl.ANY)


def f32(*shape):
    return jax.ShapeDtypeStruct(shape, jnp.float32)


def limit(mebibytes):
    return pltpu.CompilerParams(vmem_limit_bytes=mebibytes * 2**20)


def list_places(pairs, targets):
    cap = (pairs + targets) // 2 + 2 * GROUP
    cap = -(-cap // GROUP) * GROUP
    slot = 3 * 2 * cap
    groups = slot + 3 * cap
    return cap, slot, groups, groups + 2


def code_unit(blocks):
    return 1 << blocks.bit_length()


def make_plan(secs, places, targets, lists, pending, filled):
    terms, blocks = targets.shape
    total = secs * blocks
    cap, slot, groups, _ = places
    unit = code_unit(blocks)
    my_sec = lax.axis_index("sec")
    for place in range(total + 1):
        pending[place] = -1
    for region in range(3):
        filled[region] = 0

    def put(region, step, first, second, value):
        lists[2 * (region * cap + step)] = first
        lists[2 * (region * cap + step) + 1] = second
        lists[slot + region * cap + step] = value

    def take(term, carry):
        for b in range(blocks):
            target = targets[term, b]
            owner = lax.div(jnp.maximum(target, 0), blocks)
            turn = owner - my_sec
            turn = jnp.where(turn < 0, turn + secs, turn)
            own = turn == 0
            place = turn * blocks + (target - owner * blocks)
            place = jnp.where(target < 0, total, place)
            region = jnp.where(target < 0, 2, jnp.where(own, OWN, REMOTE))
            value = jnp.where(own, place, place - blocks)
            waiting, code, step = pending[place], (term * blocks + b) * unit + b, filled[region]
            put(region, step, waiting, code, value)
            filled[region] = step + jnp.where(waiting >= 0, 1, 0)
            pending[place] = jnp.where(waiting >= 0, -1, code)
        return carry

    lax.fori_loop(0, terms, take, 0)
    for region, span in ((REMOTE, range(blocks, total)), (OWN, range(blocks))):
        step = filled[region]
        for place in span:
            waiting = pending[place]
            put(region, step, jnp.maximum(waiting, 0), blocks, place - span[0])
            step = step + jnp.where(waiting >= 0, 1, 0)
        for extra in range(GROUP):
            put(region, step + extra, blocks, blocks, 0)
        lists[groups + region] = lax.div(step + GROUP - 1, GROUP)


def load_kernel(secs, places, targets, left, right, lists, left_held, right_held, pending, filled, sems):
    shares = sems.shape[1]
    each = left.shape[0] // shares
    copies = []
    for share in range(shares):
        rows = pl.ds(share * each, each)
        copies.append(pltpu.make_async_copy(left.at[rows], left_held.at[rows], sems.at[0, share]))
        copies.append(pltpu.make_async_copy(right.at[rows], right_held.at[rows], sems.at[1, share]))
    for copy in copies:
        copy.start()
    make_plan(secs, places, targets, lists, pending, filled)
    for copy in copies:
        copy.wait()


def load(secs, places, targets, left, right):
    terms, blocks = targets.shape
    return pl.pallas_call(
        functools.partial(load_kernel, secs, places),
        out_shape=(
            jax.ShapeDtypeStruct((places[-1],), jnp.int32),
            pltpu.VMEM(left.shape, left.dtype),
            pltpu.VMEM(right.shape, right.dtype),
        ),
        in_specs=[SMEM, ANY, ANY],
        out_specs=(SMEM, VMEM, VMEM),
        scratch_shapes=[
            pltpu.SMEM((secs * blocks + 1,), jnp.int32),
            pltpu.SMEM((3,), jnp.int32),
            pltpu.SemaphoreType.DMA((2, 6)),
        ],
        compiler_params=limit(2),
        cost_estimate=pl.CostEstimate(flops=0, bytes_accessed=40 * 2**20, transcendentals=0),
        name="load",
    )(
        targets,
        pltpu.with_memory_space_constraint(left, pltpu.HBM),
        pltpu.with_memory_space_constraint(right, pltpu.HBM),
    )


def square_kernel(wave, square):
    square[...] = jnp.full(square.shape, jnp.sum(wave[...] * wave[...]))


def square_sum(wave):
    return pl.pallas_call(
        square_kernel,
        out_shape=f32(8, 128),
        in_specs=[VMEM],
        out_specs=VMEM,
        compiler_params=limit(2),
        name="square_sum",
    )(wave)


def added(refs):
    total = refs[0][...]
    for ref in refs[1:]:
        total = total + ref[...]
    return total


def multiply_terms(region, places, lists, left, right, vector_bf, product, keep, send):
    cap, slot, groups, _ = places
    unit = code_unit(vector_bf.shape[0] - 1)
    my_sub = lax.axis_index("sub")
    half = keep.shape[2]
    count = lists[groups + region]
    keep[...] = jnp.zeros_like(keep)
    send[...] = jnp.zeros_like(send)

    def tile(at):
        return lax.shift_right_logical(lists[at], unit.bit_length() - 1)

    def first(group):
        for k in range(2 * GROUP):
            at = 2 * (region * cap + group * GROUP) + k
            part = jnp.dot(
                left[tile(at)], vector_bf[lists[at] & (unit - 1)], preferred_element_type=jnp.float32
            )
            product[k // 2, :, (k % 2) * half : (k % 2 + 1) * half] = part.astype(jnp.bfloat16)

    def second(group):
        for g in range(GROUP):
            at = region * cap + group * GROUP + g
            pair = jnp.concatenate([right[tile(2 * at)], right[tile(2 * at + 1)]], axis=0)
            image = jnp.dot(product[g], pair, preferred_element_type=jnp.float32)
            low, high = image[:, :half], image[:, half:]
            n = lists[slot + at]
            keep[n] += jnp.where(my_sub == 0, low, high)
            send[n] += jnp.where(my_sub == 0, high, low)

    @pl.when(count > 0)
    def _():
        first(0)

        def turn(group, carry):
            second(group - 1)
            first(group)
            return carry

        lax.fori_loop(1, count, turn, 0)
        second(count - 1)


def round_vector(vector, vector_bf):
    blocks = vector.shape[0]
    vector_bf[:blocks] = vector[...].astype(jnp.bfloat16)
    vector_bf[blocks] = jnp.zeros(vector_bf.shape[1:], jnp.bfloat16)


def start_kernel(entries, norms, places, lists, wave, *refs):
    norm_refs, (left, right, vector, keep, send, vector_bf, product) = refs[:norms], refs[norms:]
    length = jnp.sqrt(added(norm_refs)[:1, :1] / entries)
    vector[...] = wave[...] / length[None]
    round_vector(vector, vector_bf)
    multiply_terms(REMOTE, places, lists, left, right, vector_bf, product, keep, send)


def refined(entries, held, correction, sum_refs):
    sums = added(sum_refs) / entries
    along, square, own = sums[0:1, :1], sums[1:2, :1], sums[2:3, :1]
    length = jnp.sqrt((1.0 + along) * (1.0 + along) * own - 2.0 * (1.0 + along) * along + square)
    return (held[...] - (correction[...] - along[None] * held[...])) / length[None]


def resume_kernel(entries, places, lists, held, correction, *refs):
    sum_refs, (left, right, vector, keep, send, vector_bf, product) = refs[:-7], refs[-7:]
    vector[...] = refined(entries, held, correction, sum_refs)
    round_vector(vector, vector_bf)
    multiply_terms(REMOTE, places, lists, left, right, vector_bf, product, keep, send)


def own_kernel(places, lists, vector, after, left, right, keep, send, vector_bf, product):
    round_vector(vector, vector_bf)
    multiply_terms(OWN, places, lists, left, right, vector_bf, product, keep, send)


def images(kernel, slots, with_vector, name, lists, operands, left, right, after=()):
    half, rows = right.shape[1:]
    vector = operands[0]
    out = (f32(slots, rows, half),) * 2
    if with_vector:
        out = (f32(*vector.shape), *out)
    return pl.pallas_call(
        kernel,
        out_shape=out,
        in_specs=[SMEM] + [VMEM] * len(operands) + [ANY] * len(after) + [VMEM] * 2,
        out_specs=(VMEM,) * len(out),
        scratch_shapes=[
            pltpu.VMEM((vector.shape[0] + 1, rows, half), jnp.bfloat16),
            pltpu.VMEM((GROUP, rows, rows), jnp.bfloat16),
        ],
        compiler_params=limit(12),
        cost_estimate=pl.CostEstimate(flops=6 * 10**9, bytes_accessed=20 * 2**20, transcendentals=0),
        name=name,
    )(
        lists,
        *operands,
        *after,
        pltpu.with_memory_space_constraint(left, pltpu.VMEM),
        pltpu.with_memory_space_constraint(right, pltpu.VMEM),
    )


def call(kernel, out_shape, operands, name, mebibytes=4):
    return pl.pallas_call(
        kernel,
        out_shape=out_shape,
        in_specs=[VMEM] * len(operands),
        out_specs=jax.tree.map(lambda _: VMEM, out_shape),
        compiler_params=limit(mebibytes),
        name=name,
    )(*operands)


def add_kernel(*refs):
    refs[-1][...] = added(refs[:-1])


def add(parts):
    return call(add_kernel, f32(*parts[0].shape), parts, "add")


def part_kernel(aways, keep, landed, *outs):
    wholes, pieces = outs[:aways], outs[aways:]
    ops = len(pieces)
    my_op = lax.axis_index("op")
    for away in range(aways):
        wholes[away][...] = keep[away, 0] + landed[away, 0]
        for turn in range(ops):
            at = lax.rem(my_op + turn, ops)
            pieces[turn][away] = keep[away, 1, at] + landed[away, 1, at]


def part(keep, landed, aways, split):
    _, ops, rows, half = split
    shape = (aways, *split)
    outs = call(
        functools.partial(part_kernel, aways),
        (f32(ops, rows, half),) * aways + (f32(aways, rows, half),) * ops,
        (keep.reshape(shape), landed.reshape(shape)),
        "part",
    )
    return outs[:aways], outs[aways:]


def sum_kernel(parts, *refs):
    for away, out in enumerate(refs[parts:]):
        total = refs[0][away]
        for ref in refs[1:parts]:
            total = total + ref[away]
        out[...] = total


def sum_parts(parts):
    aways, rows, half = parts[0].shape
    return call(functools.partial(sum_kernel, len(parts)), (f32(rows, half),) * aways, parts, "sum_parts")


def combine_kernel(arrived, keep, landed, *refs):
    wholes, outs = refs[:arrived], refs[arrived:]
    ops = len(outs)
    my_op = lax.axis_index("op")
    for turn in range(ops):
        at = lax.rem(my_op + turn, ops)
        total = keep[0, at] + landed[0, at]
        for whole in wholes:
            total = total + whole[at]
        outs[turn][0] = total
        outs[turn][1] = keep[1, at] + landed[1, at]


def combine(keep, landed, wholes, split):
    _, ops, rows, half = split
    return call(
        functools.partial(combine_kernel, len(wholes)),
        (f32(2, rows, half),) * ops,
        (keep.reshape(split), landed.reshape(split), *wholes),
        "combine",
    )


def sigma_kernel(parts, vector, diagonal, *refs):
    pieces, arrived, (sigma, inner) = refs[:parts], refs[parts:-2], refs[-2:]
    my_op = lax.axis_index("op")
    inner_sum = jnp.float32(0)
    for side in range(2):
        total = pieces[0][side]
        for piece in pieces[1:]:
            total = total + piece[side]
        if side == 1:
            total = total + added(arrived)
        held = vector[side, my_op]
        total = diagonal[side, my_op] * held + total
        sigma[side] = total
        inner_sum += jnp.sum(held * total)
    inner[...] = jnp.full(inner.shape, inner_sum)


def sigma_share(vector, diagonal, pieces, arrived):
    _, ops, rows, half = vector.shape
    return call(
        functools.partial(sigma_kernel, len(pieces)),
        (f32(2, rows, half), f32(8, 128)),
        (vector, diagonal, *pieces, *arrived),
        "sigma",
    )


def correct_kernel(entries, ops, vector, diagonal, *refs):
    spread, theta_refs, (correction, sums, ritz) = refs[:ops], refs[ops:-3], refs[-3:]
    my_op = lax.axis_index("op")
    ritz[...] = added(theta_refs) / entries
    theta = ritz[:1, :1]
    totals = [jnp.float32(0)] * 3
    for turn in range(ops):
        at = lax.rem(my_op + ops - turn, ops)
        for side in range(2):
            held, diag = vector[side, at], diagonal[side, at]
            value = (spread[turn][side] - theta * held) / (1.0 + jnp.abs(diag - theta))
            correction[side, at] = value
            for index, term in enumerate((held * value, value * value, held * held)):
                totals[index] += jnp.sum(term)
    sums[...] = jnp.zeros_like(sums)
    for index, value in enumerate(totals):
        sums[index : index + 1] = jnp.full((1, sums.shape[1]), value)


def correct(entries, vector, diagonal, spread, thetas):
    return call(
        functools.partial(correct_kernel, entries, len(spread)),
        (f32(*vector.shape), f32(8, 128), f32(8, 128)),
        (vector, diagonal, *spread, *thetas),
        "correct",
    )


def finish_kernel(entries, sums, held, correction, *refs):
    sum_refs, ritz_refs, (out, ritz) = refs[:sums], refs[sums:-2], refs[-2:]
    out[...] = refined(entries, held, correction, sum_refs)
    for index, ref in enumerate(ritz_refs):
        ritz[index] = ref[0, 0]


def finish(entries, vector, correction, sums, ritz):
    return pl.pallas_call(
        functools.partial(finish_kernel, entries, len(sums)),
        out_shape=(f32(*vector.shape), f32(len(ritz))),
        in_specs=[VMEM] * (2 + len(sums) + len(ritz)),
        out_specs=(VMEM, SMEM),
        compiler_params=limit(4),
        name="finish",
    )(vector, correction, *sums, *ritz)


def shift(array, axis, turn):
    count = lax.axis_size(axis)
    return lax.ppermute(array, axis, [(i, (i + turn) % count) for i in range(count)])


def from_all(array, axis):
    return [array, *[shift(array, axis, k) for k in range(1, lax.axis_size(axis))]]


def per_device(wavefunction, diagonal, left_env, right_env, targets):
    ops, secs = lax.axis_size("op"), lax.axis_size("sec")
    blocks, tile, half = wavefunction.shape
    terms = left_env.shape[0]
    entries = blocks * secs * tile * tile
    left = left_env.reshape(terms * blocks, tile, tile)
    right = right_env.reshape(terms * blocks, half, tile)
    split = (2, ops, blocks * tile // ops // 2, half)
    places = list_places(terms * blocks, secs * blocks)
    aways = secs - 1
    diagonal = diagonal.reshape(split)
    norms = from_all(square_sum(wavefunction), ("sec", "sub"))
    lists, left, right = load(secs, places, targets, left, right)
    start = functools.partial(start_kernel, entries, len(norms), places)
    vector, keep, send = images(
        start, aways * blocks, True, "remote_images", lists, (wavefunction, *norms), left, right
    )
    ritz = []
    for turn_index in range(ITERS):
        wholes, shares = part(keep, shift(send, "sub", 1), aways, split)
        crossed = [shift(wholes[r - 1], "sec", r) for r in range(1, secs)]
        landed = [shift(shares[k], "op", k) for k in range(1, ops)]
        own = functools.partial(own_kernel, places)
        keep, send = images(
            own, blocks, False, "own_images", lists, (vector,), left, right, after=(wholes[0],)
        )
        reduced = sum_parts((shares[0], *landed))
        arrived = [shift(reduced[r - 1], "sec", r) for r in range(1, secs)]
        pieces = combine(keep, shift(send, "sub", 1), crossed, split)
        pieces = [pieces[0], *[shift(pieces[k], "op", k) for k in range(1, ops)]]
        held = vector.reshape(split)
        sigma, inner = sigma_share(held, diagonal, pieces, arrived)
        spread = from_all(sigma, "op")
        thetas = from_all(add(from_all(inner, ("sec", "sub"))), "op")
        correction, sums, theta = correct(entries, held, diagonal, spread, thetas)
        ritz.append(theta)
        sums = from_all(sums, ("sec", "sub"))
        correction = correction.reshape(vector.shape)
        if turn_index < ITERS - 1:
            resume = functools.partial(resume_kernel, entries, places)
            operands = (vector, correction, *sums)
            vector, keep, send = images(
                resume, aways * blocks, True, "remote_images", lists, operands, left, right
            )
    return finish(entries, vector, correction, sums, ritz)


def solution(mesh):
    placed = (
        P(("grp", "sec"), None, "sub"),
        P(("grp", "sec"), None, "sub"),
        P(("grp", "op"), "sec", None, None),
        P(("grp", "op"), "sec", "sub", None),
        P(("grp", "op"), "sec"),
    )
    return jax.shard_map(
        per_device,
        mesh=mesh,
        in_specs=placed,
        out_specs=(P(("grp", "sec"), None, "sub"), P("grp")),
        check_vma=False,
    )
```

```python
import functools

import jax
import jax.numpy as jnp
from jax import lax
from jax.experimental import pallas as pl
from jax.experimental.pallas import tpu as pltpu
from jax.sharding import PartitionSpec as P

ITERS = 2
GROUP = 4
EARLY = 3
REMOTE, OWN = 0, 1
VMEM = pl.BlockSpec(memory_space=pltpu.VMEM)
SMEM = pl.BlockSpec(memory_space=pltpu.SMEM)
ANY = pl.BlockSpec(memory_space=pl.ANY)


def f32(*shape):
    return jax.ShapeDtypeStruct(shape, jnp.float32)


def limit(mebibytes):
    return pltpu.CompilerParams(vmem_limit_bytes=mebibytes * 2**20)


def list_places(pairs, targets):
    cap = (pairs + targets) // 2 + 2 * GROUP
    cap = -(-cap // GROUP) * GROUP
    slot = 3 * 2 * cap
    groups = slot + 3 * cap
    return cap, slot, groups, groups + 2


def code_unit(blocks):
    return 1 << blocks.bit_length()


def make_plan(secs, places, targets, lists, pending, filled):
    terms, blocks = targets.shape
    total = secs * blocks
    cap, slot, groups, _ = places
    unit = code_unit(blocks)
    my_sec = lax.axis_index("sec")
    for place in range(total + 1):
        pending[place] = -1
    for region in range(3):
        filled[region] = 0

    def put(region, step, first, second, value):
        lists[2 * (region * cap + step)] = first
        lists[2 * (region * cap + step) + 1] = second
        lists[slot + region * cap + step] = value

    def take(term, carry):
        for b in range(blocks):
            target = targets[term, b]
            owner = lax.div(jnp.maximum(target, 0), blocks)
            turn = owner - my_sec
            turn = jnp.where(turn < 0, turn + secs, turn)
            own = turn == 0
            place = turn * blocks + (target - owner * blocks)
            place = jnp.where(target < 0, total, place)
            region = jnp.where(target < 0, 2, jnp.where(own, OWN, REMOTE))
            value = jnp.where(own, place, place - blocks)
            waiting, code, step = pending[place], (term * blocks + b) * unit + b, filled[region]
            put(region, step, waiting, code, value)
            filled[region] = step + jnp.where(waiting >= 0, 1, 0)
            pending[place] = jnp.where(waiting >= 0, -1, code)
        return carry

    lax.fori_loop(0, terms, take, 0)
    for region, span in ((REMOTE, range(blocks, total)), (OWN, range(blocks))):
        step = filled[region]
        for place in span:
            waiting = pending[place]
            put(region, step, jnp.maximum(waiting, 0), blocks, place - span[0])
            step = step + jnp.where(waiting >= 0, 1, 0)
        for extra in range(GROUP):
            put(region, step + extra, blocks, blocks, 0)
        lists[groups + region] = lax.div(step + GROUP - 1, GROUP)


def load_kernel(secs, places, targets, left, right, lists, left_held, right_held, pending, filled, sems):
    shares = sems.shape[1]
    each = left.shape[0] // shares
    copies = []
    for share in range(shares):
        rows = pl.ds(share * each, each)
        copies.append(pltpu.make_async_copy(left.at[rows], left_held.at[rows], sems.at[0, share]))
        copies.append(pltpu.make_async_copy(right.at[rows], right_held.at[rows], sems.at[1, share]))
    for copy in copies:
        copy.start()
    make_plan(secs, places, targets, lists, pending, filled)
    for copy in copies:
        copy.wait()


def load(secs, places, targets, left, right):
    terms, blocks = targets.shape
    return pl.pallas_call(
        functools.partial(load_kernel, secs, places),
        out_shape=(
            jax.ShapeDtypeStruct((places[-1],), jnp.int32),
            pltpu.VMEM(left.shape, left.dtype),
            pltpu.VMEM(right.shape, right.dtype),
        ),
        in_specs=[SMEM, ANY, ANY],
        out_specs=(SMEM, VMEM, VMEM),
        scratch_shapes=[
            pltpu.SMEM((secs * blocks + 1,), jnp.int32),
            pltpu.SMEM((3,), jnp.int32),
            pltpu.SemaphoreType.DMA((2, 6)),
        ],
        compiler_params=limit(2),
        cost_estimate=pl.CostEstimate(flops=0, bytes_accessed=40 * 2**20, transcendentals=0),
        name="load",
    )(
        targets,
        pltpu.with_memory_space_constraint(left, pltpu.HBM),
        pltpu.with_memory_space_constraint(right, pltpu.HBM),
    )


def square_kernel(wave, square):
    square[...] = jnp.full(square.shape, jnp.sum(wave[...] * wave[...]))


def square_sum(wave, devices):
    return pl.pallas_call(
        square_kernel,
        out_shape=f32(devices, 8, 128),
        in_specs=[VMEM],
        out_specs=VMEM,
        compiler_params=limit(2),
        name="square_sum",
    )(wave)


def added(refs):
    total = refs[0][...]
    for ref in refs[1:]:
        total = total + ref[...]
    return total


def multiply_terms(region, turns, places, lists, left, right, vector_bf, product, keep, send):
    cap, slot, groups, _ = places
    unit = code_unit(vector_bf.shape[0] - 1)
    my_sub = lax.axis_index("sub")
    half = keep.shape[2]
    count = lists[groups + region]
    begin = jnp.minimum(turns[0], count)
    end = count if turns[1] is None else jnp.minimum(turns[1], count)

    def tile(at):
        return lax.shift_right_logical(lists[at], unit.bit_length() - 1)

    def first(group):
        for k in range(2 * GROUP):
            at = 2 * (region * cap + group * GROUP) + k
            part = jnp.dot(
                left[tile(at)], vector_bf[lists[at] & (unit - 1)], preferred_element_type=jnp.float32
            )
            product[k // 2, :, (k % 2) * half : (k % 2 + 1) * half] = part.astype(jnp.bfloat16)

    def second(group):
        for g in range(GROUP):
            at = region * cap + group * GROUP + g
            pair = jnp.concatenate([right[tile(2 * at)], right[tile(2 * at + 1)]], axis=0)
            image = jnp.dot(product[g], pair, preferred_element_type=jnp.float32)
            low, high = image[:, :half], image[:, half:]
            n = lists[slot + at]
            keep[n] += jnp.where(my_sub == 0, low, high)
            send[n] += jnp.where(my_sub == 0, high, low)

    @pl.when(end > begin)
    def _():
        first(begin)

        def turn(group, carry):
            second(group - 1)
            first(group)
            return carry

        lax.fori_loop(begin + 1, end, turn, 0)
        second(end - 1)


def round_vector(vector, vector_bf):
    blocks = vector.shape[0]
    vector_bf[:blocks] = vector[...].astype(jnp.bfloat16)
    vector_bf[blocks] = jnp.zeros(vector_bf.shape[1:], jnp.bfloat16)


def remote_turns(places, lists, left, right, vector, vector_bf, keep, send, product):
    round_vector(vector, vector_bf)
    keep[...] = jnp.zeros_like(keep)
    send[...] = jnp.zeros_like(send)
    multiply_terms(REMOTE, (0, None), places, lists, left, right, vector_bf, product, keep, send)


def start_kernel(entries, places, lists, wave, norms, left, right, vector, *refs):
    length = jnp.sqrt(jnp.sum(norms[...], axis=0)[:1, :1] / entries)
    vector[...] = wave[...] / length[None]
    remote_turns(places, lists, left, right, vector, *refs)


def refined(entries, held, correction, sums):
    total = jnp.sum(sums[...], axis=0) / entries
    along, square, own = total[0:1, :1], total[1:2, :1], total[2:3, :1]
    length = jnp.sqrt((1.0 + along) * (1.0 + along) * own - 2.0 * (1.0 + along) * along + square)
    return (held[...] - (correction[...] - along[None] * held[...])) / length[None]


def resume_kernel(entries, places, lists, held, correction, sums, left, right, vector, *refs):
    vector[...] = refined(entries, held, correction, sums)
    remote_turns(places, lists, left, right, vector, *refs)


def own_first_kernel(places, lists, vector_bf, left, right, keep, send, product):
    keep[...] = jnp.zeros_like(keep)
    send[...] = jnp.zeros_like(send)
    multiply_terms(OWN, (0, EARLY), places, lists, left, right, vector_bf, product, keep, send)


def own_rest_kernel(places, lists, vector_bf, keep_in, send_in, after, left, right, keep, send, product):
    keep[...] = keep_in[...]
    send[...] = send_in[...]
    multiply_terms(OWN, (EARLY, None), places, lists, left, right, vector_bf, product, keep, send)


def images(kernel, out_shape, name, lists, operands, left, right, after=(), turns=4):
    rows = left.shape[1]
    work = turns * GROUP * 2 * 8 * rows * rows * rows // 4
    return pl.pallas_call(
        kernel,
        out_shape=out_shape,
        in_specs=[SMEM] + [VMEM] * len(operands) + [ANY] * len(after) + [VMEM] * 2,
        out_specs=(VMEM,) * len(out_shape),
        scratch_shapes=[pltpu.VMEM((GROUP, rows, rows), jnp.bfloat16)],
        compiler_params=limit(12),
        cost_estimate=pl.CostEstimate(flops=2 * work, bytes_accessed=turns * 2**20, transcendentals=0),
        name=name,
    )(
        lists,
        *operands,
        *after,
        pltpu.with_memory_space_constraint(left, pltpu.VMEM),
        pltpu.with_memory_space_constraint(right, pltpu.VMEM),
    )


def call(kernel, out_shape, operands, name, mebibytes=4):
    return pl.pallas_call(
        kernel,
        out_shape=out_shape,
        in_specs=[VMEM] * len(operands),
        out_specs=jax.tree.map(lambda _: VMEM, out_shape),
        compiler_params=limit(mebibytes),
        name=name,
    )(*operands)


def part_kernel(aways, keep, landed, *outs):
    wholes, pieces = outs[:aways], outs[aways]
    for away in range(aways):
        wholes[away][...] = keep[away, 0] + landed[away, 0]
        pieces[:, away] = keep[away, 1] + landed[away, 1]


def part(keep, landed, aways, split):
    _, ops, rows, half = split
    shape = (aways, *split)
    outs = call(
        functools.partial(part_kernel, aways),
        (f32(ops, rows, half),) * aways + (f32(ops, aways, rows, half),),
        (keep.reshape(shape), landed.reshape(shape)),
        "part",
    )
    return outs[:-1], outs[-1]


def sum_kernel(parts, *outs):
    for away, out in enumerate(outs):
        out[...] = jnp.sum(parts[:, away], axis=0)


def sum_parts(parts):
    _, aways, rows, half = parts.shape
    return call(sum_kernel, (f32(rows, half),) * aways, (parts,), "sum_parts")


def pass_kernel(value, after, out):
    out[...] = value[...]


def pass_after(value, after):
    return pl.pallas_call(
        pass_kernel,
        out_shape=f32(*value.shape),
        in_specs=[VMEM, ANY],
        out_specs=VMEM,
        compiler_params=limit(4),
        name="pass_after",
    )(value, after)


def combine_kernel(keep, landed, *refs):
    wholes, pieces = refs[:-1], refs[-1]
    total = keep[0] + landed[0]
    for whole in wholes:
        total = total + whole[...]
    pieces[:, 0] = total
    pieces[:, 1] = keep[1] + landed[1]


def combine(keep, landed, wholes, split):
    _, ops, rows, half = split
    operands = (keep.reshape(split), landed.reshape(split), *wholes)
    return call(combine_kernel, f32(ops, 2, rows, half), operands, "combine")


def sigma_kernel(vector, diagonal, pieces, *refs):
    arrived, (sigma, inner) = refs[:-2], refs[-2:]
    my_op = lax.axis_index("op")
    inner_sum = jnp.float32(0)
    for side in range(2):
        total = jnp.sum(pieces[:, side], axis=0)
        if side == 1:
            total = total + added(arrived)
        held = vector[side, my_op]
        total = diagonal[side, my_op] * held + total
        for place in range(sigma.shape[0]):
            sigma[place, side] = total
        inner_sum += jnp.sum(held * total)
    inner[...] = jnp.full(inner.shape, inner_sum)


def sigma_share(vector, diagonal, pieces, arrived, devices):
    _, ops, rows, half = vector.shape
    return call(
        sigma_kernel,
        (f32(ops, 2, rows, half), f32(devices, 8, 128)),
        (vector, diagonal, pieces, *arrived),
        "sigma",
    )


def correct_kernel(entries, vector, diagonal, sigma, thetas, correction, sums, ritz):
    ritz[...] = jnp.sum(thetas[...], axis=0) / entries
    theta = ritz[:1, :1][None]
    totals = [jnp.float32(0)] * 3
    for side in range(2):
        held, diag = vector[side], diagonal[side]
        value = (sigma[:, side] - theta * held) / (1.0 + jnp.abs(diag - theta))
        correction[side] = value
        for index, term in enumerate((held * value, value * value, held * held)):
            totals[index] += jnp.sum(term)
    sums[...] = jnp.zeros_like(sums)
    for index, value in enumerate(totals):
        sums[:, index : index + 1] = jnp.full((sums.shape[0], 1, sums.shape[2]), value)


def correct(entries, vector, diagonal, sigma, thetas, devices):
    return call(
        functools.partial(correct_kernel, entries),
        (f32(*vector.shape), f32(devices, 8, 128), f32(8, 128)),
        (vector, diagonal, sigma, thetas),
        "correct",
    )


def finish_kernel(entries, held, correction, sums, *refs):
    ritz_refs, (out, ritz) = refs[:-2], refs[-2:]
    out[...] = refined(entries, held, correction, sums)
    for index, ref in enumerate(ritz_refs):
        ritz[index] = ref[0, 0]


def finish(entries, vector, correction, sums, ritz):
    return pl.pallas_call(
        functools.partial(finish_kernel, entries),
        out_shape=(f32(*vector.shape), f32(len(ritz))),
        in_specs=[VMEM] * (3 + len(ritz)),
        out_specs=(VMEM, SMEM),
        compiler_params=limit(4),
        name="finish",
    )(vector, correction, sums, *ritz)


def shift(array, axis, turn):
    count = lax.axis_size(axis)
    return lax.ppermute(array, axis, [(i, (i + turn) % count) for i in range(count)])


def swap(array, axis):
    return lax.all_to_all(array, axis, 0, 0, tiled=True)


def per_device(wavefunction, diagonal, left_env, right_env, targets):
    ops, secs, subs = (lax.axis_size(axis) for axis in ("op", "sec", "sub"))
    blocks, tile, half = wavefunction.shape
    terms = left_env.shape[0]
    entries = blocks * secs * tile * tile
    left = left_env.reshape(terms * blocks, tile, tile)
    right = right_env.reshape(terms * blocks, half, tile)
    split = (2, ops, blocks * tile // ops // 2, half)
    places = list_places(terms * blocks, secs * blocks)
    aways = secs - 1
    rounded = jax.ShapeDtypeStruct((blocks + 1, tile, half), jnp.bfloat16)
    whole, own_out = f32(blocks, tile, half), (f32(blocks, tile, half),) * 2
    remote_out = (whole, rounded) + (f32(aways * blocks, tile, half),) * 2
    own_first = functools.partial(own_first_kernel, places)
    own_rest = functools.partial(own_rest_kernel, places)
    diagonal = diagonal.reshape(split)
    norms = swap(square_sum(wavefunction, secs * subs), ("sec", "sub"))
    lists, left, right = load(secs, places, targets, left, right)
    start = functools.partial(start_kernel, entries, places)
    vector, vector_bf, keep, send = images(
        start, remote_out, "remote_images", lists, (wavefunction, norms), left, right
    )
    ritz = []
    for turn_index in range(ITERS):
        landed = shift(send, "sub", 1)
        own_parts = images(own_first, own_out, "own_first", lists, (vector_bf,), left, right)
        wholes, shares = part(keep, landed, aways, split)
        crossed = [shift(wholes[r - 1], "sec", r) for r in range(1, secs)]
        shares = swap(shares, "op")
        keep, send = images(
            own_rest, own_out, "own_rest", lists, (vector_bf, *own_parts), left, right, after=(wholes[0],), turns=8
        )
        send = pass_after(send, crossed[-1])
        arrived = [shift(share, "sec", r) for r, share in enumerate(sum_parts(shares), 1)]
        pieces = swap(combine(keep, shift(send, "sub", 1), crossed, split), "op")
        held = vector.reshape(split)
        sigma, inner = sigma_share(held, diagonal, pieces, arrived, ops * secs * subs)
        thetas = swap(inner, ("op", "sec", "sub"))
        sigma = swap(sigma, "op")
        correction, sums, theta = correct(entries, held, diagonal, sigma, thetas, secs * subs)
        ritz.append(theta)
        sums = swap(sums, ("sec", "sub"))
        correction = correction.reshape(vector.shape)
        if turn_index < ITERS - 1:
            resume = functools.partial(resume_kernel, entries, places)
            operands = (vector, correction, sums)
            vector, vector_bf, keep, send = images(
                resume, remote_out, "remote_images", lists, operands, left, right
            )
    return finish(entries, vector, correction, sums, ritz)


def solution(mesh):
    placed = (
        P(("grp", "sec"), None, "sub"),
        P(("grp", "sec"), None, "sub"),
        P(("grp", "op"), "sec", None, None),
        P(("grp", "op"), "sec", "sub", None),
        P(("grp", "op"), "sec"),
    )
    return jax.shard_map(
        per_device,
        mesh=mesh,
        in_specs=placed,
        out_specs=(P(("grp", "sec"), None, "sub"), P("grp")),
        check_vma=False,
    )
```

```python
import functools

import jax
import jax.numpy as jnp
from jax import lax
from jax.experimental import pallas as pl
from jax.experimental.pallas import tpu as pltpu
from jax.sharding import PartitionSpec as P

ITERS = 2
GROUP = 4
EARLY = 3
REMOTE, OWN = 0, 1
VMEM = pl.BlockSpec(memory_space=pltpu.VMEM)
SMEM = pl.BlockSpec(memory_space=pltpu.SMEM)
ANY = pl.BlockSpec(memory_space=pl.ANY)


def f32(*shape):
    return jax.ShapeDtypeStruct(shape, jnp.float32)


def limit(mebibytes):
    return pltpu.CompilerParams(vmem_limit_bytes=mebibytes * 2**20)


def list_places(pairs, targets):
    cap = (pairs + targets) // 2 + 2 * GROUP
    cap = -(-cap // GROUP) * GROUP
    slot = 3 * 2 * cap
    groups = slot + 3 * cap
    return cap, slot, groups, groups + 2


def code_unit(blocks):
    return 1 << blocks.bit_length()


def make_plan(secs, places, targets, lists, pending, filled):
    terms, blocks = targets.shape
    total = secs * blocks
    cap, slot, groups, _ = places
    unit = code_unit(blocks)
    my_sec = lax.axis_index("sec")
    for place in range(total + 1):
        pending[place] = -1
    for region in range(3):
        filled[region] = 0

    def put(region, step, first, second, value):
        lists[2 * (region * cap + step)] = first
        lists[2 * (region * cap + step) + 1] = second
        lists[slot + region * cap + step] = value

    def take(term, carry):
        for b in range(blocks):
            target = targets[term, b]
            owner = lax.div(jnp.maximum(target, 0), blocks)
            turn = owner - my_sec
            turn = jnp.where(turn < 0, turn + secs, turn)
            own = turn == 0
            place = turn * blocks + (target - owner * blocks)
            place = jnp.where(target < 0, total, place)
            region = jnp.where(target < 0, 2, jnp.where(own, OWN, REMOTE))
            value = jnp.where(own, place, place - blocks)
            waiting, code, step = pending[place], (term * blocks + b) * unit + b, filled[region]
            put(region, step, waiting, code, value)
            filled[region] = step + jnp.where(waiting >= 0, 1, 0)
            pending[place] = jnp.where(waiting >= 0, -1, code)
        return carry

    lax.fori_loop(0, terms, take, 0)
    for region, span in ((REMOTE, range(blocks, total)), (OWN, range(blocks))):
        step = filled[region]
        for place in span:
            waiting = pending[place]
            put(region, step, jnp.maximum(waiting, 0), blocks, place - span[0])
            step = step + jnp.where(waiting >= 0, 1, 0)
        for extra in range(GROUP):
            put(region, step + extra, blocks, blocks, 0)
        lists[groups + region] = lax.div(step + GROUP - 1, GROUP)


def load_kernel(secs, places, targets, left, right, lists, left_held, right_held, pending, filled, sems):
    shares = sems.shape[1]
    each = left.shape[0] // shares
    copies = []
    for share in range(shares):
        rows = pl.ds(share * each, each)
        copies.append(pltpu.make_async_copy(left.at[rows], left_held.at[rows], sems.at[0, share]))
        copies.append(pltpu.make_async_copy(right.at[rows], right_held.at[rows], sems.at[1, share]))
    for copy in copies:
        copy.start()
    make_plan(secs, places, targets, lists, pending, filled)
    for copy in copies:
        copy.wait()


def load(secs, places, targets, left, right):
    terms, blocks = targets.shape
    return pl.pallas_call(
        functools.partial(load_kernel, secs, places),
        out_shape=(
            jax.ShapeDtypeStruct((places[-1],), jnp.int32),
            pltpu.VMEM(left.shape, left.dtype),
            pltpu.VMEM(right.shape, right.dtype),
        ),
        in_specs=[SMEM, ANY, ANY],
        out_specs=(SMEM, VMEM, VMEM),
        scratch_shapes=[
            pltpu.SMEM((secs * blocks + 1,), jnp.int32),
            pltpu.SMEM((3,), jnp.int32),
            pltpu.SemaphoreType.DMA((2, 6)),
        ],
        compiler_params=limit(2),
        cost_estimate=pl.CostEstimate(flops=0, bytes_accessed=40 * 2**20, transcendentals=0),
        name="load",
    )(
        targets,
        pltpu.with_memory_space_constraint(left, pltpu.HBM),
        pltpu.with_memory_space_constraint(right, pltpu.HBM),
    )


def square_kernel(wave, square):
    square[...] = jnp.full(square.shape, jnp.sum(wave[...] * wave[...]))


def square_sum(wave):
    return pl.pallas_call(
        square_kernel,
        out_shape=f32(8, 128),
        in_specs=[VMEM],
        out_specs=VMEM,
        compiler_params=limit(2),
        name="square_sum",
    )(wave)


def added(refs):
    total = refs[0][...]
    for ref in refs[1:]:
        total = total + ref[...]
    return total


def multiply_terms(region, turns, places, lists, left, right, vector_bf, product, keep, send):
    cap, slot, groups, _ = places
    unit = code_unit(vector_bf.shape[0] - 1)
    my_sub = lax.axis_index("sub")
    half = keep.shape[2]
    count = lists[groups + region]
    begin = jnp.minimum(turns[0], count)
    end = count if turns[1] is None else jnp.minimum(turns[1], count)

    def tile(at):
        return lax.shift_right_logical(lists[at], unit.bit_length() - 1)

    def first(group):
        for k in range(2 * GROUP):
            at = 2 * (region * cap + group * GROUP) + k
            part = jnp.dot(
                left[tile(at)], vector_bf[lists[at] & (unit - 1)], preferred_element_type=jnp.float32
            )
            product[k // 2, :, (k % 2) * half : (k % 2 + 1) * half] = part.astype(jnp.bfloat16)

    def second(group):
        for g in range(GROUP):
            at = region * cap + group * GROUP + g
            pair = jnp.concatenate([right[tile(2 * at)], right[tile(2 * at + 1)]], axis=0)
            image = jnp.dot(product[g], pair, preferred_element_type=jnp.float32)
            low, high = image[:, :half], image[:, half:]
            n = lists[slot + at]
            keep[n] += jnp.where(my_sub == 0, low, high)
            send[n] += jnp.where(my_sub == 0, high, low)

    @pl.when(end > begin)
    def _():
        first(begin)

        def turn(group, carry):
            second(group - 1)
            first(group)
            return carry

        lax.fori_loop(begin + 1, end, turn, 0)
        second(end - 1)


def round_vector(vector, vector_bf):
    blocks = vector.shape[0]
    vector_bf[:blocks] = vector[...].astype(jnp.bfloat16)
    vector_bf[blocks] = jnp.zeros(vector_bf.shape[1:], jnp.bfloat16)


def remote_turns(places, lists, left, right, vector, vector_bf, keep, send, product):
    round_vector(vector, vector_bf)
    keep[...] = jnp.zeros_like(keep)
    send[...] = jnp.zeros_like(send)
    multiply_terms(REMOTE, (0, None), places, lists, left, right, vector_bf, product, keep, send)


def start_kernel(entries, norms, places, lists, wave, *refs):
    norm_refs, (left, right, vector, *refs) = refs[:norms], refs[norms:]
    length = jnp.sqrt(added(norm_refs)[:1, :1] / entries)
    vector[...] = wave[...] / length[None]
    remote_turns(places, lists, left, right, vector, *refs)


def refined(entries, held, correction, sum_refs):
    total = added(sum_refs) / entries
    along, square, own = total[0:1, :1], total[1:2, :1], total[2:3, :1]
    length = jnp.sqrt((1.0 + along) * (1.0 + along) * own - 2.0 * (1.0 + along) * along + square)
    return (held[...] - (correction[...] - along[None] * held[...])) / length[None]


def resume_kernel(entries, sums, places, lists, held, correction, *refs):
    sum_refs, (left, right, vector, *refs) = refs[:sums], refs[sums:]
    vector[...] = refined(entries, held, correction, sum_refs)
    remote_turns(places, lists, left, right, vector, *refs)


def own_first_kernel(places, lists, vector_bf, left, right, keep, send, product):
    keep[...] = jnp.zeros_like(keep)
    send[...] = jnp.zeros_like(send)
    multiply_terms(OWN, (0, EARLY), places, lists, left, right, vector_bf, product, keep, send)


def own_rest_kernel(places, lists, vector_bf, keep_in, send_in, after, left, right, keep, send, product):
    keep[...] = keep_in[...]
    send[...] = send_in[...]
    multiply_terms(OWN, (EARLY, None), places, lists, left, right, vector_bf, product, keep, send)


def images(kernel, out_shape, name, lists, operands, left, right, after=(), turns=4):
    rows = left.shape[1]
    work = turns * GROUP * 2 * 8 * rows * rows * rows // 4
    return pl.pallas_call(
        kernel,
        out_shape=out_shape,
        in_specs=[SMEM] + [VMEM] * len(operands) + [ANY] * len(after) + [VMEM] * 2,
        out_specs=(VMEM,) * len(out_shape),
        scratch_shapes=[pltpu.VMEM((GROUP, rows, rows), jnp.bfloat16)],
        compiler_params=limit(12),
        cost_estimate=pl.CostEstimate(flops=2 * work, bytes_accessed=turns * 2**20, transcendentals=0),
        name=name,
    )(
        lists,
        *operands,
        *after,
        pltpu.with_memory_space_constraint(left, pltpu.VMEM),
        pltpu.with_memory_space_constraint(right, pltpu.VMEM),
    )


def call(kernel, out_shape, operands, name, mebibytes=4):
    return pl.pallas_call(
        kernel,
        out_shape=out_shape,
        in_specs=[VMEM] * len(operands),
        out_specs=jax.tree.map(lambda _: VMEM, out_shape),
        compiler_params=limit(mebibytes),
        name=name,
    )(*operands)


def add_kernel(*refs):
    refs[-1][...] = added(refs[:-1])


def add(parts):
    return call(add_kernel, f32(*parts[0].shape), parts, "add")


def part_kernel(aways, keep, landed, *outs):
    for away in range(aways):
        for side in range(2):
            outs[2 * away + side][...] = keep[away, side] + landed[away, side]


def part(keep, landed, aways):
    blocks, rows, half = keep.shape
    shape = (aways, 2, blocks // aways // 2, rows, half)
    return call(
        functools.partial(part_kernel, aways),
        (f32(*shape[2:]),) * (2 * aways),
        (keep.reshape(shape), landed.reshape(shape)),
        "part",
    )


def pass_kernel(count, *refs):
    for value, out in zip(refs[:count], refs[count + 1 :]):
        out[...] = value[...]


def pass_after(values, after):
    return pl.pallas_call(
        functools.partial(pass_kernel, len(values)),
        out_shape=tuple(f32(*value.shape) for value in values),
        in_specs=[VMEM] * len(values) + [ANY],
        out_specs=(VMEM,) * len(values),
        compiler_params=limit(4),
        name="pass_after",
    )(*values, after)


def combine_kernel(arrived, earlier, side, vector, diagonal, keep, landed, *refs):
    wholes, outs = refs[:arrived], refs[arrived + earlier :]
    ops = len(outs)
    rows, half = keep.shape[2:]
    my_op = lax.axis_index("op")
    held = vector[side, my_op]
    inner = diagonal[side, my_op] * held * held
    for turn in range(ops):
        at = lax.rem(my_op + turn, ops)
        total = keep[side, at] + landed[side, at]
        for whole in wholes:
            total = total + whole[at]
        outs[turn][:rows] = total
        inner = inner + vector[side, at] * total
    share = jnp.sum(inner.reshape(rows // 8, 8, half), axis=0)
    for turn in range(ops):
        outs[turn][rows:] = share


def combine(side, vector, diagonal, keep, landed, wholes, earlier):
    _, ops, rows, half = vector.shape
    operands = [vector, diagonal, keep.reshape(vector.shape), landed.reshape(vector.shape)]
    operands += [whole.reshape(ops, rows, half) for whole in wholes]
    return pl.pallas_call(
        functools.partial(combine_kernel, len(wholes), len(earlier), side),
        out_shape=(f32(rows + 8, half),) * ops,
        in_specs=[VMEM] * len(operands) + [ANY] * len(earlier),
        out_specs=(VMEM,) * ops,
        compiler_params=limit(4),
        name="combine",
    )(*operands, *earlier)


def sigma_kernel(vector, diagonal, *refs):
    pieces, (sigma, inner) = refs[:-2], refs[-2:]
    ops = len(pieces) // 2
    rows = sigma.shape[1]
    my_op = lax.axis_index("op")
    shares = jnp.zeros((8, sigma.shape[2]), jnp.float32)
    for side in range(2):
        total = added(pieces[side * ops : (side + 1) * ops])
        sigma[side] = diagonal[side, my_op] * vector[side, my_op] + total[:rows]
        shares = shares + total[rows:]
    inner[...] = jnp.full(inner.shape, jnp.sum(shares))


def sigma_share(vector, diagonal, pieces):
    _, ops, rows, half = vector.shape
    return call(
        sigma_kernel, (f32(2, rows, half), f32(8, 128)), (vector, diagonal, *pieces), "sigma"
    )


def correct_kernel(entries, ops, vector, diagonal, *refs):
    spread, theta_refs, (correction, sums, ritz) = refs[:ops], refs[ops:-3], refs[-3:]
    my_op = lax.axis_index("op")
    ritz[...] = added(theta_refs) / entries
    theta = ritz[:1, :1]
    totals = [0.0] * 3
    for turn in range(ops):
        at = lax.rem(my_op + ops - turn, ops)
        for side in range(2):
            held, diag = vector[side, at], diagonal[side, at]
            value = (spread[turn][side] - theta * held) / (1.0 + jnp.abs(diag - theta))
            correction[side, at] = value
            for index, term in enumerate((held * value, value * value, held * held)):
                totals[index] = totals[index] + term
    sums[...] = jnp.zeros_like(sums)
    for index, value in enumerate(totals):
        sums[index : index + 1] = jnp.full((1, sums.shape[1]), jnp.sum(value))


def correct(entries, vector, diagonal, spread, thetas):
    return call(
        functools.partial(correct_kernel, entries, len(spread)),
        (f32(*vector.shape), f32(8, 128), f32(8, 128)),
        (vector, diagonal, *spread, *thetas),
        "correct",
    )


def finish_kernel(entries, sums, held, correction, *refs):
    sum_refs, ritz_refs, (out, ritz) = refs[:sums], refs[sums:-2], refs[-2:]
    out[...] = refined(entries, held, correction, sum_refs)
    for index, ref in enumerate(ritz_refs):
        ritz[index] = ref[0, 0]


def finish(entries, vector, correction, sums, ritz):
    return pl.pallas_call(
        functools.partial(finish_kernel, entries, len(sums)),
        out_shape=(f32(*vector.shape), f32(len(ritz))),
        in_specs=[VMEM] * (2 + len(sums) + len(ritz)),
        out_specs=(VMEM, SMEM),
        compiler_params=limit(4),
        name="finish",
    )(vector, correction, *sums, *ritz)


def shift(array, axis, turn):
    count = lax.axis_size(axis)
    return lax.ppermute(array, axis, [(i, (i + turn) % count) for i in range(count)])


def from_all(array, axis):
    return [array, *[shift(array, axis, k) for k in range(1, lax.axis_size(axis))]]


def sector_sums(array):
    return from_all(add(from_all(array, "sub")), "sec")


def per_device(wavefunction, diagonal, left_env, right_env, targets):
    ops, secs = lax.axis_size("op"), lax.axis_size("sec")
    blocks, tile, half = wavefunction.shape
    terms = left_env.shape[0]
    entries = blocks * secs * tile * tile
    left = left_env.reshape(terms * blocks, tile, tile)
    right = right_env.reshape(terms * blocks, half, tile)
    split = (2, ops, blocks * tile // ops // 2, half)
    places = list_places(terms * blocks, secs * blocks)
    aways = secs - 1
    rounded = jax.ShapeDtypeStruct((blocks + 1, tile, half), jnp.bfloat16)
    whole, own_out = f32(blocks, tile, half), (f32(blocks, tile, half),) * 2
    remote_out = (whole, rounded) + (f32(aways * blocks, tile, half),) * 2
    own_first = functools.partial(own_first_kernel, places)
    own_rest = functools.partial(own_rest_kernel, places)
    diagonal = diagonal.reshape(split)
    norms = sector_sums(square_sum(wavefunction))
    lists, left, right = load(secs, places, targets, left, right)
    start = functools.partial(start_kernel, entries, len(norms), places)
    vector, vector_bf, keep, send = images(
        start, remote_out, "remote_images", lists, (wavefunction, *norms), left, right
    )
    ritz = []
    for turn_index in range(ITERS):
        landed = shift(send, "sub", 1)
        own_parts = images(own_first, own_out, "own_first", lists, (vector_bf,), left, right)
        halves = part(keep, landed, aways)
        crossed = [shift(halves[2 * r - 2], "sec", r) for r in range(1, secs)]
        keep, send = images(
            own_rest, own_out, "own_rest", lists, (vector_bf, *own_parts), left, right, after=(halves[0],), turns=8
        )
        send, *others = pass_after((send, *halves[1::2]), crossed[-1])
        crossed_later = [shift(other, "sec", r) for r, other in enumerate(others, 1)]
        landed = shift(send, "sub", 1)
        held = vector.reshape(split)
        pieces = []
        for side, wholes in enumerate((crossed, crossed_later)):
            outs = combine(side, held, diagonal, keep, landed, wholes, pieces[1:])
            pieces += [outs[0], *[shift(outs[k], "op", k) for k in range(1, ops)]]
        sigma, inner = sigma_share(held, diagonal, pieces)
        spread = from_all(sigma, "op")
        thetas = sector_sums(inner)
        correction, sums, theta = correct(entries, held, diagonal, spread, thetas)
        ritz.append(theta)
        sums = sector_sums(sums)
        correction = correction.reshape(vector.shape)
        if turn_index < ITERS - 1:
            resume = functools.partial(resume_kernel, entries, len(sums), places)
            operands = (vector, correction, *sums)
            vector, vector_bf, keep, send = images(
                resume, remote_out, "remote_images", lists, operands, left, right
            )
    return finish(entries, vector, correction, sums, ritz)


def solution(mesh):
    placed = (
        P(("grp", "sec"), None, "sub"),
        P(("grp", "sec"), None, "sub"),
        P(("grp", "op"), "sec", None, None),
        P(("grp", "op"), "sec", "sub", None),
        P(("grp", "op"), "sec"),
    )
    return jax.shard_map(
        per_device,
        mesh=mesh,
        in_specs=placed,
        out_specs=(P(("grp", "sec"), None, "sub"), P("grp")),
        check_vma=False,
    )
```
